32 devices in a mesh: dp: 4 (over y, x), seq: 8 (over z, core).
Axes of the slice: x: 2, y: 2, z: 4, core: 2. Of those that a mesh axis runs over, the one named last changes fastest.
Arguments:
- qkv: bfloat16 [3, 4, 2, 512, 4096], P(None, 'dp', None, 'seq'), may hold values from -4 to 4
- master: float32 [4, 4096], P(None, 'dp'), may hold values from -0.9 to 5.2
- moment_one: float32 [4, 4096], P(None, 'dp'), may hold values from -3 to 3
- moment_two: float32 [4, 4096], P(None, 'dp'), may hold values from 0.25 to 4
- grads: float32 [4, 4096], P(None, 'dp'), may hold values from -8 to 8
Outputs:
- attended: bfloat16 [4, 2, 512, 4096], P('dp', None, 'seq')
- updated: float32 [4, 4096], P(None, 'dp')
- first_moment: float32 [4, 4096], P(None, 'dp')
- second_moment: float32 [4, 4096], P(None, 'dp')
The draws below stay inside these ranges and needn't reach their ends.
All inputs are finite; a program needn't handle non-finite values.
Results may differ from the reference program's by a relative error of at most 0.0011.
The reference program's roundings to bfloat16 on the way count: a program that leaves them out, or rounds other values in their place, can miss the bound.
Values may be sent and summed in bfloat16 or wider, within the bound.
No kernel may reach another device: no remote copies, remote signals or barrier semaphores. Data moves between devices by JAX's collectives and lax.ppermute only.
A program may use at most 64 MiB of HBM per device.

```python
import math
import jax
import jax.numpy as jnp
from jax import lax

D = 4096
HEADS = 32
HD = 128
SEQS = 2
OPT_STEP = 10
PATCHES = 512
N_DP = 4


def draw_qkv(key, part):
    key_one = jax.random.fold_in(key, 11)
    result = jax.random.normal(key_one, (3, N_DP, SEQS, PATCHES, D), jnp.float32)
    return jnp.clip(result, -4.0, 4.0).astype(jnp.bfloat16)


def draw_master(key, part):
    key_two = jax.random.fold_in(key, 22)
    key_three = jax.random.fold_in(key, 23)
    gains = jax.random.uniform(key_two, (2, D), jnp.float32, 0.7, 1.4)
    biases = jnp.clip(0.3 * jax.random.normal(key_three, (2, D), jnp.float32), -0.9, 0.9)
    return jnp.stack([gains[0], biases[0], gains[1], biases[1]]).astype(jnp.float32)


def block_scale(own_key, extent, pieces, low, high):
    loudness, own = 1.0, jax.random.fold_in(own_key, 6)
    for position, shards_of in pieces:
        heights = jnp.exp(jax.random.uniform(jax.random.fold_in(own, position), (shards_of,), jnp.float32, low / len(pieces), high / len(pieces)))
        loudness = loudness * jnp.repeat(heights, extent[position] // shards_of).reshape([-1 if axis == position else 1 for axis in range(len(extent))])
    return loudness


def scatter_about(own_key, shape, scale, limit, cuts=(), kind=jnp.bfloat16):
    values = scale * jax.random.normal(own_key, shape, jnp.float32)
    if cuts:
        values = values * block_scale(own_key, shape, cuts, -0.22, 0.18)
    return jnp.clip(values, -limit, limit).astype(kind)


def setup_inputs(seed: int = 0) -> dict:
    key_of = jax.random.split(jax.random.key(seed), 6)
    qkv = draw_qkv(jax.random.fold_in(key_of[5], 71), 0)
    master = draw_master(jax.random.fold_in(key_of[5], 71), 0)
    moment_one = scatter_about(key_of[2], (4, D), 0.5, 3.0, ((1, 4),), jnp.float32)
    moment_two = jnp.clip(jnp.exp(math.log(4.0) - 2.7725887 * jax.random.uniform(key_of[3], (4, D), jnp.float32) ** block_scale(key_of[3], (4, D), ((1, 4),), -0.2, 0.2)), 0.25, 4.0)
    grads = scatter_about(key_of[4], (4, D), 2.0, 8.0, ((1, 4),), jnp.float32)
    return dict(qkv=qkv, master=master, moment_one=moment_one, moment_two=moment_two, grads=grads)


BETA_ONE = 0.9
BETA_TWO = 0.95
RATE = 0.02
DECAY = 0.1
EPSILON = 1e-08

def adamw(master, moment_one, moment_two, grads):
    first_moment = BETA_ONE * moment_one + (1.0 - BETA_ONE) * grads
    second_moment = BETA_TWO * moment_two + (1.0 - BETA_TWO) * grads * grads
    first_hat = first_moment / (1.0 - BETA_ONE ** OPT_STEP)
    second_hat = second_moment / (1.0 - BETA_TWO ** OPT_STEP)
    updated = master - RATE * (first_hat / (jnp.sqrt(second_hat) + EPSILON) + DECAY * master)
    return (updated, first_moment, second_moment)

def normalize(values, gain_row, bias_row):
    row_count = values.shape[0]
    head_count = values.shape[1] // HD
    grouped = values.astype(jnp.float32).reshape(row_count, head_count, HD)
    centre = lax.optimization_barrier(jnp.mean(grouped, axis=-1, keepdims=True))
    spread = lax.optimization_barrier(jnp.mean((grouped - centre) ** 2, axis=-1, keepdims=True))
    scaled = (grouped - centre) / jnp.sqrt(spread + 1e-06)
    scaled = scaled * gain_row.reshape(head_count, HD) + bias_row.reshape(head_count, HD)
    return scaled.reshape(row_count, head_count * HD).astype(jnp.bfloat16)

def reference(qkv, master, moment_one, moment_two, grads):
    updated, first_moment, second_moment = adamw(master, moment_one, moment_two, grads)
    layer_bf = updated.astype(jnp.bfloat16)
    layer_bf = lax.optimization_barrier(layer_bf)
    layer_full = layer_bf.astype(jnp.float32)
    sample_count = N_DP * SEQS
    samples = qkv.reshape(3, sample_count, PATCHES, D)
    scale_value = HD ** (-0.5)

    def one_sample(sample_id):
        span_rows = lax.dynamic_index_in_dim(samples, sample_id, 1, keepdims=False)
        queries = normalize(span_rows[0], layer_full[0], layer_full[1])
        key_rows = normalize(span_rows[1], layer_full[2], layer_full[3])
        query_heads = queries.reshape(PATCHES, HEADS, HD).transpose(1, 0, 2)
        key_heads = key_rows.reshape(PATCHES, HEADS, HD).transpose(1, 0, 2)
        value_heads = span_rows[2].reshape(PATCHES, HEADS, HD).transpose(1, 0, 2)

        def one_head(triple):
            query_one, key_one, value_one = triple
            scores = jnp.dot(query_one, key_one.T, preferred_element_type=jnp.float32) * scale_value
            probs = jax.nn.softmax(scores, axis=-1).astype(jnp.bfloat16)
            return jnp.dot(probs, value_one, preferred_element_type=jnp.float32).astype(jnp.bfloat16)
        head_outs = lax.map(one_head, (query_heads, key_heads, value_heads))
        return head_outs.transpose(1, 0, 2).reshape(PATCHES, HEADS * HD)
    outputs = lax.map(one_sample, jnp.arange(sample_count, dtype=jnp.int32))
    attended = outputs.reshape(N_DP, SEQS, PATCHES, D)
    return (attended, updated, first_moment, second_moment)
```

```python
import functools

import jax
import jax.numpy as jnp
from jax import lax
from jax.experimental import pallas as pl
from jax.experimental.pallas import tpu as pltpu
from jax.sharding import PartitionSpec as P

HEADS = 32
HD = 128
OPT_STEP = 10

BETA_ONE = 0.9
BETA_TWO = 0.95
RATE = 0.02
DECAY = 0.1
EPSILON = 1e-08

LOG2E = 1.4426950408889634
ANY = pl.BlockSpec(memory_space=pl.ANY)
VMEM = pl.BlockSpec(memory_space=pltpu.VMEM)


def adamw(master, moment_one, moment_two, grads):
    first_moment = BETA_ONE * moment_one + (1.0 - BETA_ONE) * grads
    second_moment = BETA_TWO * moment_two + (1.0 - BETA_TWO) * grads * grads
    first_hat = first_moment / (1.0 - BETA_ONE**OPT_STEP)
    second_hat = second_moment / (1.0 - BETA_TWO**OPT_STEP)
    updated = master - RATE * (first_hat / (jnp.sqrt(second_hat) + EPSILON) + DECAY * master)
    return (updated, first_moment, second_moment)


def own_columns(layer, dp_count, seq_count, width):
    shard_cols = layer.shape[1]
    assert shard_cols % width == 0
    rounds = []
    for owner in range(dp_count):
        wanted = [
            (dp, seq)
            for seq in range(seq_count)
            if seq * width // shard_cols == owner
            for dp in range(dp_count)
            if dp != owner
        ]
        for place, (dp, seq) in enumerate(wanted):
            turn, source = divmod(place, seq_count)
            while len(rounds) <= turn:
                rounds.append([])
            rounds[turn].append((owner * seq_count + source, dp * seq_count + seq))
    first_col = lax.axis_index("seq") * width
    mine = lax.axis_index("dp") == first_col // shard_cols
    found = jnp.where(mine, layer, jnp.zeros_like(layer))
    for pairs in rounds:
        found = found + lax.ppermute(layer, ("dp", "seq"), pairs)
    return lax.dynamic_slice_in_dim(found, first_col % shard_cols, width, 1)


def pack_kernel(sample, count, width, source, *rest):
    outs, sems = rest[:count], rest[count]
    me = lax.axis_index("seq")
    copies = []
    for slot in range(count):
        first = pl.multiple_of(lax.bitwise_xor(me, slot) * width, width)
        copies.append(
            pltpu.make_async_copy(
                source.at[:, 0, sample, :, pl.ds(first, width)], outs[slot], sems.at[slot]
            )
        )
    for copy in copies:
        copy.start()
    for copy in copies:
        copy.wait()


def pack(qkv, sample, count, width):
    rows = qkv.shape[3]
    shape = jax.ShapeDtypeStruct((3, rows, width), qkv.dtype)
    return pl.pallas_call(
        functools.partial(pack_kernel, sample, count, width),
        out_shape=[shape] * count,
        in_specs=[ANY],
        out_specs=[ANY] * count,
        scratch_shapes=[pltpu.SemaphoreType.DMA((count,))],
        name="pack",
    )(qkv)


def normed(rows, gain, bias):
    grouped = rows.astype(jnp.float32)
    centred = grouped - jnp.mean(grouped, axis=-1, keepdims=True)
    spread = jnp.mean(centred * centred, axis=-1, keepdims=True)
    return (centred * lax.rsqrt(spread + 1e-06) * gain + bias).astype(jnp.bfloat16)


def attend_kernel(count, block, layer, *rest):
    arrived, outs = rest[:count], rest[count : 2 * count]
    rows, width = outs[0].shape
    per_block = max(1, block // rows)
    for head in range(width // HD):
        cols = slice(head * HD, (head + 1) * HD)
        gains = layer[:, cols].astype(jnp.float32)
        keys = jnp.concatenate([normed(a[1, :, cols], gains[2:3], gains[3:4]) for a in arrived])
        values = jnp.concatenate([a[2, :, cols] for a in arrived])
        for first in range(0, count, per_block):
            slots = range(first, first + per_block)
            queries = jnp.concatenate(
                [normed(arrived[slot][0, :, cols], gains[0:1], gains[1:2]) for slot in slots]
            )
            scores = lax.dot_general(
                queries, keys, (((1,), (1,)), ((), ())), preferred_element_type=jnp.float32
            )
            top = jnp.max(scores, axis=-1, keepdims=True)
            raised = jnp.exp2((scores - top) * (HD**-0.5 * LOG2E))
            total = jnp.sum(raised, axis=-1, keepdims=True)
            probs = (raised * (1.0 / total)).astype(jnp.bfloat16)
            result = jnp.dot(probs, values, preferred_element_type=jnp.float32)
            result = result.astype(jnp.bfloat16)
            for place, slot in enumerate(slots):
                outs[slot][:, cols] = result[place * rows : (place + 1) * rows]


def attend(layer, arrived):
    count = len(arrived)
    _, rows, width = arrived[0].shape
    patches = count * rows
    return pl.pallas_call(
        functools.partial(attend_kernel, count, 256),
        out_shape=[jax.ShapeDtypeStruct((rows, width), jnp.bfloat16)] * count,
        in_specs=[VMEM] * (1 + count),
        out_specs=[VMEM] * count,
        compiler_params=pltpu.CompilerParams(vmem_limit_bytes=32 * 1024 * 1024),
        cost_estimate=pl.CostEstimate(
            flops=4 * patches * patches * width,
            bytes_accessed=8 * patches * width,
            transcendentals=patches * patches * (width // HD),
        ),
        name="attend",
    )(layer, *arrived)


def unpack_kernel(samples, count, width, *rest):
    parts, out, sems = rest[: samples * count], rest[samples * count], rest[samples * count + 1]
    me = lax.axis_index("seq")
    copies = []
    for sample in range(samples):
        for slot in range(count):
            first = pl.multiple_of(lax.bitwise_xor(me, slot) * width, width)
            place = sample * count + slot
            copies.append(
                pltpu.make_async_copy(
                    parts[place], out.at[0, sample, :, pl.ds(first, width)], sems.at[place]
                )
            )
    for copy in copies:
        copy.start()
    for copy in copies:
        copy.wait()


def unpack(parts, samples, count):
    rows, width = parts[0].shape
    return pl.pallas_call(
        functools.partial(unpack_kernel, samples, count, width),
        out_shape=jax.ShapeDtypeStruct((1, samples, rows, width * count), parts[0].dtype),
        in_specs=[ANY] * len(parts),
        out_specs=ANY,
        scratch_shapes=[pltpu.SemaphoreType.DMA((len(parts),))],
        name="unpack",
    )(*parts)


def exchange(parts, order):
    count = len(parts)
    landed = list(parts)
    for slot in order:
        pairs = [(place, place ^ slot) for place in range(count)]
        landed[slot] = lax.ppermute(parts[slot], "seq", pairs)
    return landed


def shards(dp_count, seq_count, qkv, master, moment_one, moment_two, grads):
    samples = qkv.shape[2]
    width = qkv.shape[4] // seq_count
    order = list(range(seq_count - 1, 0, -1))
    landed = [exchange(pack(qkv, sample, seq_count, width), order) for sample in range(samples)]
    updated, first_moment, second_moment = adamw(master, moment_one, moment_two, grads)
    layer = own_columns(updated.astype(jnp.bfloat16), dp_count, seq_count, width)
    parts = []
    for sample in range(samples):
        parts += exchange(attend(layer, landed[sample]), order)
    attended = unpack(parts, samples, seq_count)
    return (attended, updated, first_moment, second_moment)


def solution(mesh):
    placed = (
        P(None, "dp", None, "seq", None),
        P(None, "dp"),
        P(None, "dp"),
        P(None, "dp"),
        P(None, "dp"),
    )
    return jax.shard_map(
        functools.partial(shards, mesh.shape["dp"], mesh.shape["seq"]),
        mesh=mesh,
        in_specs=placed,
        out_specs=(P("dp", None, "seq", None), P(None, "dp"), P(None, "dp"), P(None, "dp")),
        check_vma=False,
    )
```

```python
import functools

import jax
import jax.numpy as jnp
from jax import lax
from jax.experimental import pallas as pl
from jax.experimental.pallas import tpu as pltpu
from jax.sharding import PartitionSpec as P

HEADS = 32
HD = 128
OPT_STEP = 10

BETA_ONE = 0.9
BETA_TWO = 0.95
RATE = 0.02
DECAY = 0.1
EPSILON = 1e-08

LOG2E = 1.4426950408889634
ANY = pl.BlockSpec(memory_space=pl.ANY)
VMEM = pl.BlockSpec(memory_space=pltpu.VMEM)


def adamw(master, moment_one, moment_two, grads):
    first_moment = BETA_ONE * moment_one + (1.0 - BETA_ONE) * grads
    second_moment = BETA_TWO * moment_two + (1.0 - BETA_TWO) * grads * grads
    first_hat = first_moment / (1.0 - BETA_ONE**OPT_STEP)
    second_hat = second_moment / (1.0 - BETA_TWO**OPT_STEP)
    updated = master - RATE * (first_hat / (jnp.sqrt(second_hat) + EPSILON) + DECAY * master)
    return (updated, first_moment, second_moment)


def own_columns(layer, dp_count, seq_count, width):
    shard_cols = layer.shape[1]
    assert shard_cols % width == 0
    rounds = []
    for owner in range(dp_count):
        wanted = [
            (dp, seq)
            for seq in range(seq_count)
            if seq * width // shard_cols == owner
            for dp in range(dp_count)
            if dp != owner
        ]
        for place, (dp, seq) in enumerate(wanted):
            turn, source = divmod(place, seq_count)
            while len(rounds) <= turn:
                rounds.append([])
            rounds[turn].append((owner * seq_count + source, dp * seq_count + seq))
    first_col = lax.axis_index("seq") * width
    mine = lax.axis_index("dp") == first_col // shard_cols
    found = jnp.where(mine, layer, jnp.zeros_like(layer))
    for pairs in rounds:
        found = found + lax.ppermute(layer, ("dp", "seq"), pairs)
    return lax.dynamic_slice_in_dim(found, first_col % shard_cols, width, 1)


def pack_kernel(sample, count, width, source, *rest):
    outs, sems = rest[:count], rest[count]
    me = lax.axis_index("seq")
    copies = []
    for slot in range(count):
        first = pl.multiple_of(lax.bitwise_xor(me, slot) * width, width)
        copies.append(
            pltpu.make_async_copy(
                source.at[:, 0, sample, :, pl.ds(first, width)], outs[slot], sems.at[slot]
            )
        )
    for copy in copies:
        copy.start()
    for copy in copies:
        copy.wait()


def pack(qkv, sample, count, width):
    rows = qkv.shape[3]
    shape = jax.ShapeDtypeStruct((3, rows, width), qkv.dtype)
    return pl.pallas_call(
        functools.partial(pack_kernel, sample, count, width),
        out_shape=[shape] * count,
        in_specs=[ANY],
        out_specs=[VMEM] * count,
        scratch_shapes=[pltpu.SemaphoreType.DMA((count,))],
        name="pack",
    )(qkv)


def normed(rows, gain, bias):
    grouped = rows.astype(jnp.float32)
    centred = grouped - jnp.mean(grouped, axis=-1, keepdims=True)
    spread = jnp.mean(centred * centred, axis=-1, keepdims=True)
    return (centred * lax.rsqrt(spread + 1e-06) * gain + bias).astype(jnp.bfloat16)


def attend_kernel(count, block, layer, *rest):
    arrived, outs = rest[:count], rest[count : 2 * count]
    rows, width = outs[0].shape
    per_block = max(1, block // rows)
    for head in range(width // HD):
        cols = slice(head * HD, (head + 1) * HD)
        gains = layer[:, cols].astype(jnp.float32)
        keys = jnp.concatenate([normed(a[1, :, cols], gains[2:3], gains[3:4]) for a in arrived])
        values = jnp.concatenate([a[2, :, cols] for a in arrived])
        for first in range(0, count, per_block):
            slots = range(first, first + per_block)
            queries = jnp.concatenate(
                [normed(arrived[slot][0, :, cols], gains[0:1], gains[1:2]) for slot in slots]
            )
            scores = lax.dot_general(
                queries, keys, (((1,), (1,)), ((), ())), preferred_element_type=jnp.float32
            )
            top = jnp.max(scores, axis=-1, keepdims=True)
            raised = jnp.exp2((scores - top) * (HD**-0.5 * LOG2E))
            total = jnp.sum(raised, axis=-1, keepdims=True)
            probs = (raised * (1.0 / total)).astype(jnp.bfloat16)
            result = jnp.dot(probs, values, preferred_element_type=jnp.float32)
            result = result.astype(jnp.bfloat16)
            for place, slot in enumerate(slots):
                outs[slot][:, cols] = result[place * rows : (place + 1) * rows]


def attend(layer, arrived):
    count = len(arrived)
    _, rows, width = arrived[0].shape
    patches = count * rows
    return pl.pallas_call(
        functools.partial(attend_kernel, count, 256),
        out_shape=[jax.ShapeDtypeStruct((rows, width), jnp.bfloat16)] * count,
        in_specs=[VMEM] * (1 + count),
        out_specs=[VMEM] * count,
        compiler_params=pltpu.CompilerParams(vmem_limit_bytes=32 * 1024 * 1024),
        cost_estimate=pl.CostEstimate(
            flops=4 * patches * patches * width,
            bytes_accessed=8 * patches * width,
            transcendentals=patches * patches * (width // HD),
        ),
        name="attend",
    )(layer, *arrived)


def unpack_kernel(samples, count, width, *rest):
    parts, out, sems = rest[: samples * count], rest[samples * count], rest[samples * count + 1]
    me = lax.axis_index("seq")
    copies = []
    for sample in range(samples):
        for slot in range(count):
            first = pl.multiple_of(lax.bitwise_xor(me, slot) * width, width)
            place = sample * count + slot
            copies.append(
                pltpu.make_async_copy(
                    parts[place], out.at[0, sample, :, pl.ds(first, width)], sems.at[place]
                )
            )
    for copy in copies:
        copy.start()
    for copy in copies:
        copy.wait()


def unpack(parts, samples, count):
    rows, width = parts[0].shape
    return pl.pallas_call(
        functools.partial(unpack_kernel, samples, count, width),
        out_shape=jax.ShapeDtypeStruct((1, samples, rows, width * count), parts[0].dtype),
        in_specs=[VMEM] * len(parts),
        out_specs=ANY,
        scratch_shapes=[pltpu.SemaphoreType.DMA((len(parts),))],
        name="unpack",
    )(*parts)


def exchange(parts, order):
    count = len(parts)
    landed = list(parts)
    for slot in order:
        pairs = [(place, place ^ slot) for place in range(count)]
        landed[slot] = lax.ppermute(parts[slot], "seq", pairs)
    return landed


def shards(dp_count, seq_count, qkv, master, moment_one, moment_two, grads):
    samples = qkv.shape[2]
    width = qkv.shape[4] // seq_count
    order = list(range(seq_count - 1, 0, -1))
    landed = [exchange(pack(qkv, sample, seq_count, width), order) for sample in range(samples)]
    updated, first_moment, second_moment = adamw(master, moment_one, moment_two, grads)
    layer = own_columns(updated.astype(jnp.bfloat16), dp_count, seq_count, width)
    parts = []
    for sample in range(samples):
        parts += exchange(attend(layer, landed[sample]), order)
    attended = unpack(parts, samples, seq_count)
    return (attended, updated, first_moment, second_moment)


def solution(mesh):
    placed = (
        P(None, "dp", None, "seq", None),
        P(None, "dp"),
        P(None, "dp"),
        P(None, "dp"),
        P(None, "dp"),
    )
    return jax.shard_map(
        functools.partial(shards, mesh.shape["dp"], mesh.shape["seq"]),
        mesh=mesh,
        in_specs=placed,
        out_specs=(P("dp", None, "seq", None), P(None, "dp"), P(None, "dp"), P(None, "dp")),
        check_vma=False,
    )
```

```python
import functools

import jax
import jax.numpy as jnp
from jax import lax
from jax.experimental import pallas as pl
from jax.experimental.pallas import tpu as pltpu
from jax.sharding import PartitionSpec as P

HEADS = 32
HD = 128
OPT_STEP = 10

BETA_ONE = 0.9
BETA_TWO = 0.95
RATE = 0.02
DECAY = 0.1
EPSILON = 1e-08

LOG2E = 1.4426950408889634
ANY = pl.BlockSpec(memory_space=pl.ANY)
VMEM = pl.BlockSpec(memory_space=pltpu.VMEM)


def adamw(master, moment_one, moment_two, grads):
    first_moment = BETA_ONE * moment_one + (1.0 - BETA_ONE) * grads
    second_moment = BETA_TWO * moment_two + (1.0 - BETA_TWO) * grads * grads
    first_hat = first_moment / (1.0 - BETA_ONE**OPT_STEP)
    second_hat = second_moment / (1.0 - BETA_TWO**OPT_STEP)
    updated = master - RATE * (first_hat / (jnp.sqrt(second_hat) + EPSILON) + DECAY * master)
    return (updated, first_moment, second_moment)


def own_columns(layer, dp_count, seq_count, width):
    shard_cols = layer.shape[1]
    assert shard_cols % width == 0
    rounds = []
    for owner in range(dp_count):
        wanted = [
            (dp, seq)
            for seq in range(seq_count)
            if seq * width // shard_cols == owner
            for dp in range(dp_count)
            if dp != owner
        ]
        for place, (dp, seq) in enumerate(wanted):
            turn, source = divmod(place, seq_count)
            while len(rounds) <= turn:
                rounds.append([])
            rounds[turn].append((owner * seq_count + source, dp * seq_count + seq))
    first_col = lax.axis_index("seq") * width
    mine = lax.axis_index("dp") == first_col // shard_cols
    found = jnp.where(mine, layer, jnp.zeros_like(layer))
    for pairs in rounds:
        found = found + lax.ppermute(layer, ("dp", "seq"), pairs)
    return lax.dynamic_slice_in_dim(found, first_col % shard_cols, width, 1)


def pack_kernel(sample, slots, width, source, *rest):
    outs, sems = rest[:-1], rest[-1]
    me = lax.axis_index("seq")
    copies = []
    for place, slot in enumerate(slots):
        first = pl.multiple_of(lax.bitwise_xor(me, slot) * width, width)
        copies.append(
            pltpu.make_async_copy(
                source.at[:, 0, sample, :, pl.ds(first, width)], outs[place], sems.at[place]
            )
        )
    for copy in copies:
        copy.start()
    for copy in copies:
        copy.wait()


def pack(qkv, sample, slots, width):
    rows = qkv.shape[3]
    count = len(slots)
    shape = jax.ShapeDtypeStruct((3, rows, width), qkv.dtype)
    return pl.pallas_call(
        functools.partial(pack_kernel, sample, slots, width),
        out_shape=[shape] * count,
        in_specs=[ANY],
        out_specs=[VMEM] * count,
        scratch_shapes=[pltpu.SemaphoreType.DMA((count,))],
        name="pack",
    )(qkv)


def normed(rows, gain, bias):
    grouped = rows.astype(jnp.float32)
    centred = grouped - jnp.mean(grouped, axis=-1, keepdims=True)
    spread = jnp.mean(centred * centred, axis=-1, keepdims=True)
    return (centred * lax.rsqrt(spread + 1e-06) * gain + bias).astype(jnp.bfloat16)


def attend_kernel(count, block, layer, *rest):
    arrived, outs = rest[:count], rest[count : 2 * count]
    rows, width = outs[0].shape
    per_block = max(1, block // rows)
    for head in range(width // HD):
        cols = slice(head * HD, (head + 1) * HD)
        gains = layer[:, cols].astype(jnp.float32)
        keys = jnp.concatenate([normed(a[1, :, cols], gains[2:3], gains[3:4]) for a in arrived])
        values = jnp.concatenate([a[2, :, cols] for a in arrived])
        for first in range(0, count, per_block):
            slots = range(first, first + per_block)
            queries = jnp.concatenate(
                [normed(arrived[slot][0, :, cols], gains[0:1], gains[1:2]) for slot in slots]
            )
            scores = lax.dot_general(
                queries, keys, (((1,), (1,)), ((), ())), preferred_element_type=jnp.float32
            )
            top = jnp.max(scores, axis=-1, keepdims=True)
            raised = jnp.exp2((scores - top) * (HD**-0.5 * LOG2E))
            total = jnp.sum(raised, axis=-1, keepdims=True)
            probs = (raised * (1.0 / total)).astype(jnp.bfloat16)
            result = jnp.dot(probs, values, preferred_element_type=jnp.float32)
            result = result.astype(jnp.bfloat16)
            for place, slot in enumerate(slots):
                outs[slot][:, cols] = result[place * rows : (place + 1) * rows]


def attend(layer, arrived):
    count = len(arrived)
    _, rows, width = arrived[0].shape
    patches = count * rows
    return pl.pallas_call(
        functools.partial(attend_kernel, count, 256),
        out_shape=[jax.ShapeDtypeStruct((rows, width), jnp.bfloat16)] * count,
        in_specs=[VMEM] * (1 + count),
        out_specs=[VMEM] * count,
        compiler_params=pltpu.CompilerParams(vmem_limit_bytes=32 * 1024 * 1024),
        cost_estimate=pl.CostEstimate(
            flops=4 * patches * patches * width,
            bytes_accessed=8 * patches * width,
            transcendentals=patches * patches * (width // HD),
        ),
        name="attend",
    )(layer, *arrived)


def unpack_kernel(samples, slots, width, *rest):
    parts, out, sems = rest[:-2], rest[-2], rest[-1]
    me = lax.axis_index("seq")
    copies = []
    for sample in range(samples):
        for slot in slots:
            first = pl.multiple_of(lax.bitwise_xor(me, slot) * width, width)
            place = len(copies)
            copies.append(
                pltpu.make_async_copy(
                    parts[place], out.at[0, sample, :, pl.ds(first, width)], sems.at[place]
                )
            )
    for copy in copies:
        copy.start()
    for copy in copies:
        copy.wait()


def unpack(parts, samples, slots):
    rows, width = parts[0].shape
    return pl.pallas_call(
        functools.partial(unpack_kernel, samples, slots, width),
        out_shape=jax.ShapeDtypeStruct((1, samples, rows, width * len(slots)), parts[0].dtype),
        in_specs=[VMEM] * len(parts),
        out_specs=ANY,
        scratch_shapes=[pltpu.SemaphoreType.DMA((len(parts),))],
        name="unpack",
    )(*parts)


def exchange(parts, slots):
    landed = []
    for part, slot in zip(parts, slots, strict=True):
        pairs = [(place, place ^ slot) for place in range(len(slots))]
        landed.append(lax.ppermute(part, "seq", pairs) if slot else part)
    return landed


def shards(dp_count, seq_count, qkv, master, moment_one, moment_two, grads):
    samples = qkv.shape[2]
    width = qkv.shape[4] // seq_count
    half = seq_count // 2
    far, near = list(range(half, seq_count)), list(range(1, half))
    slots_in = slots_out = [slot for pair in zip(far, near + [0]) for slot in pair]
    landed = [exchange(pack(qkv, sample, slots_in, width), slots_in) for sample in range(samples)]
    updated, first_moment, second_moment = adamw(master, moment_one, moment_two, grads)
    layer = own_columns(updated.astype(jnp.bfloat16), dp_count, seq_count, width)
    outs = []
    for sample in range(samples):
        result = attend(layer, landed[sample])
        outs += exchange([result[slots_in.index(slot)] for slot in slots_out], slots_out)
    attended = unpack(outs, samples, slots_out)
    return (attended, updated, first_moment, second_moment)


def solution(mesh):
    placed = (
        P(None, "dp", None, "seq", None),
        P(None, "dp"),
        P(None, "dp"),
        P(None, "dp"),
        P(None, "dp"),
    )
    return jax.shard_map(
        functools.partial(shards, mesh.shape["dp"], mesh.shape["seq"]),
        mesh=mesh,
        in_specs=placed,
        out_specs=(P("dp", None, "seq", None), P(None, "dp"), P(None, "dp"), P(None, "dp")),
        check_vma=False,
    )
```

```python
import functools

import jax
import jax.numpy as jnp
from jax import lax
from jax.experimental import pallas as pl
from jax.experimental.pallas import tpu as pltpu
from jax.sharding import PartitionSpec as P

HEADS = 32
HD = 128
OPT_STEP = 10

BETA_ONE = 0.9
BETA_TWO = 0.95
RATE = 0.02
DECAY = 0.1
EPSILON = 1e-08

LOG2E = 1.4426950408889634
ANY = pl.BlockSpec(memory_space=pl.ANY)
VMEM = pl.BlockSpec(memory_space=pltpu.VMEM)


def adamw(master, moment_one, moment_two, grads):
    first_moment = BETA_ONE * moment_one + (1.0 - BETA_ONE) * grads
    second_moment = BETA_TWO * moment_two + (1.0 - BETA_TWO) * grads * grads
    first_hat = first_moment / (1.0 - BETA_ONE**OPT_STEP)
    second_hat = second_moment / (1.0 - BETA_TWO**OPT_STEP)
    updated = master - RATE * (first_hat / (jnp.sqrt(second_hat) + EPSILON) + DECAY * master)
    return (updated, first_moment, second_moment)


def own_columns(layer, dp_count, seq_count, width):
    shard_cols = layer.shape[1]
    assert shard_cols % width == 0
    rounds = []
    for owner in range(dp_count):
        wanted = [
            (dp, seq)
            for seq in range(seq_count)
            if seq * width // shard_cols == owner
            for dp in range(dp_count)
            if dp != owner
        ]
        for place, (dp, seq) in enumerate(wanted):
            turn, source = divmod(place, seq_count)
            while len(rounds) <= turn:
                rounds.append([])
            rounds[turn].append((owner * seq_count + source, dp * seq_count + seq))
    first_col = lax.axis_index("seq") * width
    mine = lax.axis_index("dp") == first_col // shard_cols
    found = jnp.where(mine, layer, jnp.zeros_like(layer))
    for pairs in rounds:
        found = found + lax.ppermute(layer, ("dp", "seq"), pairs)
    return lax.dynamic_slice_in_dim(found, first_col % shard_cols, width, 1)


def pack_kernel(sample, slots, width, source, *rest):
    outs, sems = rest[:-1], rest[-1]
    me = lax.axis_index("seq")
    copies = []
    for place, slot in enumerate(slots):
        first = pl.multiple_of(lax.bitwise_xor(me, slot) * width, width)
        copies.append(
            pltpu.make_async_copy(
                source.at[:, 0, sample, :, pl.ds(first, width)], outs[place], sems.at[place]
            )
        )
    for copy in copies:
        copy.start()
    for copy in copies:
        copy.wait()


def pack(qkv, sample, slots, width):
    rows = qkv.shape[3]
    count = len(slots)
    shape = jax.ShapeDtypeStruct((3, rows, width), qkv.dtype)
    return pl.pallas_call(
        functools.partial(pack_kernel, sample, slots, width),
        out_shape=[shape] * count,
        in_specs=[ANY],
        out_specs=[VMEM] * count,
        scratch_shapes=[pltpu.SemaphoreType.DMA((count,))],
        compiler_params=pltpu.CompilerParams(vmem_limit_bytes=4 * 1024 * 1024),
        name="pack",
    )(qkv)


def normed(rows, gain, bias):
    grouped = rows.astype(jnp.float32)
    centred = grouped - jnp.mean(grouped, axis=-1, keepdims=True)
    spread = jnp.mean(centred * centred, axis=-1, keepdims=True)
    return (centred * lax.rsqrt(spread + 1e-06) * gain + bias).astype(jnp.bfloat16)


def attend_kernel(sample, slots, block, layer, qkv, *rest):
    count = len(slots)
    half = count // 2
    landed, rest = dict(zip(slots[:-1], rest[: count - 1], strict=True)), rest[count - 1 :]
    given, rest = (rest[:half], rest[half:]) if sample else ([], rest)
    outs = rest[:count]
    held, sem = rest[count:]
    _, rows, width = held.shape
    own = pl.multiple_of(lax.axis_index("seq") * width, width)
    copy = pltpu.make_async_copy(qkv.at[:, 0, sample, :, pl.ds(own, width)], held, sem)
    copy.start()
    for before, out in zip(given, outs):
        out[:sample] = before[...]
    landed[0] = held
    per_block = max(1, block // rows)
    for head in range(width // HD):
        cols = slice(head * HD, (head + 1) * HD)
        gains = layer[:, cols].astype(jnp.float32)
        others = [
            normed(landed[slot][1, :, cols], gains[2:3], gains[3:4]) for slot in range(1, count)
        ]
        if head == 0:
            copy.wait()
        keys = jnp.concatenate([normed(held[1, :, cols], gains[2:3], gains[3:4])] + others)
        values = jnp.concatenate([landed[slot][2, :, cols] for slot in range(count)])
        for first in range(0, count, per_block):
            here = range(first, min(first + per_block, count))
            queries = jnp.concatenate(
                [normed(landed[slot][0, :, cols], gains[0:1], gains[1:2]) for slot in here]
            )
            scores = lax.dot_general(
                queries, keys, (((1,), (1,)), ((), ())), preferred_element_type=jnp.float32
            )
            top = jnp.max(scores, axis=-1, keepdims=True)
            raised = jnp.exp2((scores - top) * (HD**-0.5 * LOG2E))
            total = jnp.sum(raised, axis=-1, keepdims=True)
            probs = (raised * (1.0 / total)).astype(jnp.bfloat16)
            result = jnp.dot(probs, values, preferred_element_type=jnp.float32)
            result = result.astype(jnp.bfloat16)
            for place, slot in enumerate(here):
                there = sample if slot < half else 0
                outs[slot][there, :, cols] = result[place * rows : (place + 1) * rows]


def attend(sample, slots, layer, qkv, arrived, given):
    count = len(slots)
    half = count // 2
    _, rows, width = arrived[0].shape
    patches = count * rows
    return pl.pallas_call(
        functools.partial(attend_kernel, sample, slots, 512),
        out_shape=[jax.ShapeDtypeStruct((sample + 1, rows, width), jnp.bfloat16)] * half
        + [jax.ShapeDtypeStruct((1, rows, width), jnp.bfloat16)] * half,
        in_specs=[VMEM, ANY] + [VMEM] * (count - 1 + len(given)),
        out_specs=[VMEM] * count,
        scratch_shapes=[pltpu.VMEM((3, rows, width), jnp.bfloat16), pltpu.SemaphoreType.DMA(())],
        compiler_params=pltpu.CompilerParams(vmem_limit_bytes=16 * 1024 * 1024),
        cost_estimate=pl.CostEstimate(
            flops=4 * patches * patches * width,
            bytes_accessed=8 * patches * width,
            transcendentals=patches * patches * (width // HD),
        ),
        name="attend",
    )(layer, qkv, *arrived, *given)


def unpack_kernel(places, width, *rest):
    parts, out, sems = rest[:-2], rest[-2], rest[-1]
    me = lax.axis_index("seq")
    copies = []
    for place, (sample, samples, slot) in enumerate(places):
        first = pl.multiple_of(lax.bitwise_xor(me, slot) * width, width)
        there = out.at[0, pl.ds(sample, samples), :, pl.ds(first, width)]
        copies.append(pltpu.make_async_copy(parts[place], there, sems.at[place]))
    for copy in copies:
        copy.start()
    for copy in copies:
        copy.wait()


def unpack(parts, places, shape):
    return pl.pallas_call(
        functools.partial(unpack_kernel, places, parts[0].shape[2]),
        out_shape=jax.ShapeDtypeStruct(shape, parts[0].dtype),
        in_specs=[VMEM] * len(parts),
        out_specs=ANY,
        scratch_shapes=[pltpu.SemaphoreType.DMA((len(parts),))],
        compiler_params=pltpu.CompilerParams(vmem_limit_bytes=4 * 1024 * 1024),
        name="unpack",
    )(*parts)


def exchange(parts, slots):
    landed = []
    for part, slot in zip(parts, slots, strict=True):
        pairs = [(place, place ^ slot) for place in range(lax.axis_size("seq"))]
        landed.append(lax.ppermute(part, "seq", pairs) if slot else part)
    return landed


def mixed(one, other):
    return [slot for pair in zip(one, other, strict=True) for slot in pair]


def shards(dp_count, seq_count, qkv, master, moment_one, moment_two, grads):
    samples = qkv.shape[2]
    width = qkv.shape[4] // seq_count
    half = seq_count // 2
    far, near = list(range(half, seq_count)), list(range(1, half))
    turned = far[half // 2 :] + far[: half // 2]
    slots_in = [mixed(far if sample else turned, near + [0]) for sample in range(samples)]
    landed = [
        exchange(pack(qkv, sample, slots_in[sample][:-1], width), slots_in[sample][:-1])
        for sample in range(samples)
    ]
    updated, first_moment, second_moment = adamw(master, moment_one, moment_two, grads)
    layer = own_columns(updated.astype(jnp.bfloat16), dp_count, seq_count, width)
    outs, near_out = {}, []
    for sample in range(samples):
        result = attend(sample, slots_in[sample], layer, qkv, landed[sample], near_out)
        near_out = result[:half]
        outs.update({(sample, 1, slot): result[slot] for slot in far})
    outs.update({(0, samples, slot): part for slot, part in enumerate(near_out)})
    places = [(sample, 1, slot) for sample in range(samples) for slot in far]
    places += [(0, samples, slot) for slot in near[1:] + near[:1] + [0]]
    parts = exchange([outs[place] for place in places], [place[2] for place in places])
    attended = unpack(parts, places, (1, *qkv.shape[2:]))
    return (attended, updated, first_moment, second_moment)


def solution(mesh):
    placed = (
        P(None, "dp", None, "seq", None),
        P(None, "dp"),
        P(None, "dp"),
        P(None, "dp"),
        P(None, "dp"),
    )
    return jax.shard_map(
        functools.partial(shards, mesh.shape["dp"], mesh.shape["seq"]),
        mesh=mesh,
        in_specs=placed,
        out_specs=(P("dp", None, "seq", None), P(None, "dp"), P(None, "dp"), P(None, "dp")),
        check_vma=False,
    )
```

```python
import functools

import jax
import jax.numpy as jnp
from jax import lax
from jax.experimental import pallas as pl
from jax.experimental.pallas import tpu as pltpu
from jax.sharding import PartitionSpec as P

HEADS = 32
HD = 128
OPT_STEP = 10

BETA_ONE = 0.9
BETA_TWO = 0.95
RATE = 0.02
DECAY = 0.1
EPSILON = 1e-08

LOG2E = 1.4426950408889634
ANY = pl.BlockSpec(memory_space=pl.ANY)
HBM = pl.BlockSpec(memory_space=pltpu.HBM)
VMEM = pl.BlockSpec(memory_space=pltpu.VMEM)


def adamw(master, moment_one, moment_two, grads):
    first_moment = BETA_ONE * moment_one + (1.0 - BETA_ONE) * grads
    second_moment = BETA_TWO * moment_two + (1.0 - BETA_TWO) * grads * grads
    first_hat = first_moment / (1.0 - BETA_ONE**OPT_STEP)
    second_hat = second_moment / (1.0 - BETA_TWO**OPT_STEP)
    updated = master - RATE * (first_hat / (jnp.sqrt(second_hat) + EPSILON) + DECAY * master)
    return (updated, first_moment, second_moment)


def own_columns(layer, dp_count, seq_count, width):
    shard_cols = layer.shape[1]
    assert shard_cols % width == 0
    rounds = []
    for owner in range(dp_count):
        wanted = [
            (dp, seq)
            for seq in range(seq_count)
            if seq * width // shard_cols == owner
            for dp in range(dp_count)
            if dp != owner
        ]
        for place, (dp, seq) in enumerate(wanted):
            turn, source = divmod(place, seq_count)
            while len(rounds) <= turn:
                rounds.append([])
            rounds[turn].append((owner * seq_count + source, dp * seq_count + seq))
    first_col = lax.axis_index("seq") * width
    mine = lax.axis_index("dp") == first_col // shard_cols
    found = jnp.where(mine, layer, jnp.zeros_like(layer))
    for pairs in rounds:
        found = found + lax.ppermute(layer, ("dp", "seq"), pairs)
    return lax.dynamic_slice_in_dim(found, first_col % shard_cols, width, 1)


def spans(chunk):
    runs = []
    for place, (sample, head) in enumerate(chunk):
        if runs and runs[-1][0] == sample and runs[-1][1] + runs[-1][2] == head:
            runs[-1][2] += 1
        else:
            runs.append([sample, head, 1, place])
    return [
        (sample, first * HD, slice(place * HD, (place + count) * HD), count * HD)
        for sample, first, count, place in runs
    ]


def pack_kernel(chunk, slots, width, source, *rest):
    outs, sems = rest[:-1], rest[-1]
    me = lax.axis_index("seq")
    copies = []
    for out, slot in zip(outs, slots, strict=True):
        for sample, first, cols, size in spans(chunk):
            start = pl.multiple_of(lax.bitwise_xor(me, slot) * width + first, HD)
            part = source.at[:, 0, sample, :, pl.ds(start, size)]
            copies.append(pltpu.make_async_copy(part, out.at[:, :, cols], sems.at[len(copies)]))
    for copy in copies:
        copy.start()
    for copy in copies:
        copy.wait()


def pack(qkv, chunk, slots, width):
    shape = jax.ShapeDtypeStruct((3, qkv.shape[3], len(chunk) * HD), qkv.dtype)
    count = len(slots) * len(spans(chunk))
    return pl.pallas_call(
        functools.partial(pack_kernel, chunk, slots, width),
        out_shape=[shape] * len(slots),
        in_specs=[HBM],
        out_specs=[VMEM] * len(slots),
        scratch_shapes=[pltpu.SemaphoreType.DMA((count,))],
        compiler_params=pltpu.CompilerParams(vmem_limit_bytes=62 * 1024 * 1024),
        name="pack",
    )(qkv)


def normed(rows, gain, bias):
    grouped = rows.astype(jnp.float32)
    centred = grouped - jnp.mean(grouped, axis=-1, keepdims=True)
    spread = jnp.mean(centred * centred, axis=-1, keepdims=True)
    return (centred * lax.rsqrt(spread + 1e-06) * gain + bias).astype(jnp.bfloat16)


def attend_kernel(chunk, slots, width, fetch, layer, qkv, *rest):
    count = len(slots)
    half = count // 2
    landed, rest = dict(zip(slots[:-1], rest[: count - 1], strict=True)), rest[count - 1 :]
    held, sems = rest[-2:]
    outs = rest[-2 - count : -2]
    given = rest[: -2 - count]
    rows = held.shape[2]
    copies = []
    own = lax.axis_index("seq") * width
    for sample, first, cols, size in spans(chunk):
        start = pl.multiple_of(own + first, HD)
        part = qkv.at[:, 0, sample, :, pl.ds(start, size)]
        copies.append(pltpu.make_async_copy(part, held.at[0, :, :, cols], sems.at[len(copies)]))
    if fetch:
        for slot in range(1, count):
            copies.append(pltpu.make_async_copy(landed[slot], held.at[slot], sems.at[len(copies)]))
            landed[slot] = held.at[slot]
    landed[0] = held.at[0]
    for copy in copies:
        copy.start()
    done = 0
    for out, before in zip(outs, given):
        done = before.shape[1]
        out[:, :done] = before[...]
    if fetch:
        for copy in copies:
            copy.wait()
    for place, (_, head) in enumerate(chunk):
        cols = slice(place * HD, (place + 1) * HD)
        gains = layer[:, head * HD : (head + 1) * HD].astype(jnp.float32)
        others = [
            normed(landed[slot][1, :, cols], gains[2:3], gains[3:4]) for slot in range(1, count)
        ]
        if place == 0 and not fetch:
            for copy in copies:
                copy.wait()
        keys = jnp.concatenate([normed(landed[0][1, :, cols], gains[2:3], gains[3:4])] + others)
        values = jnp.concatenate([landed[slot][2, :, cols] for slot in range(count)])
        per_block = max(1, 512 // rows)
        for first in range(0, count, per_block):
            here = range(first, min(first + per_block, count))
            queries = jnp.concatenate(
                [normed(landed[slot][0, :, cols], gains[0:1], gains[1:2]) for slot in here]
            )
            scores = lax.dot_general(
                queries, keys, (((1,), (1,)), ((), ())), preferred_element_type=jnp.float32
            )
            top = jnp.max(scores, axis=-1, keepdims=True)
            raised = jnp.exp2((scores - top) * (HD**-0.5 * LOG2E))
            total = jnp.sum(raised, axis=-1, keepdims=True)
            probs = (raised * (1.0 / total)).astype(jnp.bfloat16)
            result = jnp.dot(probs, values, preferred_element_type=jnp.float32)
            result = result.astype(jnp.bfloat16)
            for turn, slot in enumerate(here):
                part = result[turn * rows : (turn + 1) * rows]
                if slot < half:
                    outs[slot][:, done + place * HD : done + (place + 1) * HD] = part
                else:
                    outs[slot][:, cols] = part


def attend(chunk, slots, width, fetch, layer, qkv, arrived, given):
    count = len(slots)
    half = count // 2
    _, rows, cols = arrived[0].shape
    patches = count * rows
    before = given[0].shape[1] if given else 0
    outs = pl.pallas_call(
        functools.partial(attend_kernel, chunk, slots, width, fetch),
        out_shape=[jax.ShapeDtypeStruct((rows, before + cols), jnp.bfloat16)] * half
        + [jax.ShapeDtypeStruct((rows, cols), jnp.bfloat16)] * half,
        in_specs=[VMEM, HBM]
        + [ANY if fetch else VMEM] * (count - 1)
        + [VMEM] * len(given),
        out_specs=[VMEM] * count,
        scratch_shapes=[
            pltpu.VMEM((count if fetch else 1, 3, rows, cols), jnp.bfloat16),
            pltpu.SemaphoreType.DMA((len(spans(chunk)) + count,)),
        ],
        compiler_params=pltpu.CompilerParams(vmem_limit_bytes=16 * 1024 * 1024),
        cost_estimate=pl.CostEstimate(
            flops=4 * patches * patches * cols,
            bytes_accessed=8 * patches * cols,
            transcendentals=patches * patches * len(chunk),
        ),
        name="attend",
    )(layer, qkv, *arrived, *given)
    return list(outs[:half]), list(outs[half:])


def unpack_kernel(places, width, *rest):
    parts, out, sems = rest[: len(places)], rest[-2], rest[-1]
    me = lax.axis_index("seq")
    copies = []
    for part, (chunk, slot) in zip(parts, places, strict=True):
        for sample, first, cols, size in spans(chunk):
            start = pl.multiple_of(lax.bitwise_xor(me, slot) * width + first, HD)
            there = out.at[0, sample, :, pl.ds(start, size)]
            copies.append(pltpu.make_async_copy(part.at[:, cols], there, sems.at[len(copies)]))
    for copy in copies:
        copy.start()
    for copy in copies:
        copy.wait()


def unpack(parts, places, width, shape):
    return pl.pallas_call(
        functools.partial(unpack_kernel, places, width),
        out_shape=jax.ShapeDtypeStruct(shape, parts[0].dtype),
        in_specs=[VMEM] * len(parts),
        out_specs=ANY,
        scratch_shapes=[
            pltpu.SemaphoreType.DMA((sum(len(spans(chunk)) for chunk, _ in places),))
        ],
        compiler_params=pltpu.CompilerParams(vmem_limit_bytes=4 * 1024 * 1024),
        name="unpack",
    )(*parts)


def swap(part, slot):
    if slot == 0:
        return part
    return lax.ppermute(part, "seq", [(place, place ^ slot) for place in range(lax.axis_size("seq"))])


def mixed(one, other):
    return [slot for pair in zip(one, other, strict=True) for slot in pair]


def shards(dp_count, seq_count, qkv, master, moment_one, moment_two, grads):
    width = qkv.shape[4] // seq_count
    half = seq_count // 2
    far, near = list(range(half, seq_count)), list(range(1, half))
    turned = far[half // 2 :] + far[: half // 2]
    pairs = [(sample, head) for sample in range(qkv.shape[2]) for head in range(width // HD)]
    cut = len(pairs) - max(1, len(pairs) // 2)
    chunks = [pairs[:cut], pairs[cut:]]
    orders = [
        [turned[0], near[0], turned[1]] + mixed(turned[2:], near[1:]) + [0],
        mixed(far, near + [0]),
    ]
    landed = []
    for chunk, slots in zip(chunks, orders, strict=True):
        parts = []
        for some in [slots[:1], slots[1:-1]] if chunk is chunks[0] else [slots[:-1]]:
            parts += pack(qkv, chunk, some, width)
        landed.append([swap(part, slot) for part, slot in zip(parts, slots[:-1], strict=True)])
    updated, first_moment, second_moment = adamw(master, moment_one, moment_two, grads)
    layer = own_columns(updated.astype(jnp.bfloat16), dp_count, seq_count, width)
    parts, places, near_out = [], [], []
    for turn, (chunk, slots) in enumerate(zip(chunks, orders, strict=True)):
        near_out, far_out = attend(
            chunk, slots, width, turn == 0, layer, qkv, landed[turn], near_out
        )
        parts += [swap(out, slot) for out, slot in zip(far_out, far, strict=True)]
        places += [(chunk, slot) for slot in far]
    for slot in near[1:] + near[:1] + [0]:
        parts.append(swap(near_out[slot], slot))
        places.append((pairs, slot))
    attended = unpack(parts, places, width, (1, *qkv.shape[2:]))
    return (attended, updated, first_moment, second_moment)


def solution(mesh):
    placed = (
        P(None, "dp", None, "seq", None),
        P(None, "dp"),
        P(None, "dp"),
        P(None, "dp"),
        P(None, "dp"),
    )
    return jax.shard_map(
        functools.partial(shards, mesh.shape["dp"], mesh.shape["seq"]),
        mesh=mesh,
        in_specs=placed,
        out_specs=(P("dp", None, "seq", None), P(None, "dp"), P(None, "dp"), P(None, "dp")),
        check_vma=False,
    )
```

```python
import functools

import jax
import jax.numpy as jnp
from jax import lax
from jax.experimental import pallas as pl
from jax.experimental.pallas import tpu as pltpu
from jax.sharding import PartitionSpec as P

HEADS = 32
HD = 128
OPT_STEP = 10

BETA_ONE = 0.9
BETA_TWO = 0.95
RATE = 0.02
DECAY = 0.1
EPSILON = 1e-08

LOG2E = 1.4426950408889634
ANY = pl.BlockSpec(memory_space=pl.ANY)
HBM = pl.BlockSpec(memory_space=pltpu.HBM)
VMEM = pl.BlockSpec(memory_space=pltpu.VMEM)


def adamw(master, moment_one, moment_two, grads):
    first_moment = BETA_ONE * moment_one + (1.0 - BETA_ONE) * grads
    second_moment = BETA_TWO * moment_two + (1.0 - BETA_TWO) * grads * grads
    first_hat = first_moment / (1.0 - BETA_ONE**OPT_STEP)
    second_hat = second_moment / (1.0 - BETA_TWO**OPT_STEP)
    updated = master - RATE * (first_hat / (jnp.sqrt(second_hat) + EPSILON) + DECAY * master)
    return (updated, first_moment, second_moment)


def own_columns(layer, dp_count, seq_count, width):
    shard_cols = layer.shape[1]
    assert shard_cols % width == 0
    rounds = [[] for _ in range(dp_count - 1)]
    for seq in range(seq_count):
        owner = seq * width // shard_cols
        for turn, pairs in enumerate(rounds):
            other = (owner + turn + 1) % dp_count
            pairs.append((owner * seq_count + seq, other * seq_count + seq))
    first_col = lax.axis_index("seq") * width
    mine = lax.axis_index("dp") == first_col // shard_cols
    found = jnp.where(mine, layer, jnp.zeros_like(layer))
    for pairs in rounds:
        found = found + lax.ppermute(layer, ("dp", "seq"), pairs)
    return lax.dynamic_slice_in_dim(found, first_col % shard_cols, width, 1)


def spans(chunk):
    runs = []
    for place, (sample, head) in enumerate(chunk):
        if runs and runs[-1][0] == sample and runs[-1][1] + runs[-1][2] == head:
            runs[-1][2] += 1
        else:
            runs.append([sample, head, 1, place])
    return [
        (sample, first * HD, slice(place * HD, (place + count) * HD), count * HD)
        for sample, first, count, place in runs
    ]


def cut_out(qkv, chunk, slot, width):
    own = lax.bitwise_xor(lax.axis_index("seq"), slot) * width
    runs = [
        lax.dynamic_slice_in_dim(qkv[:, 0, sample], own + first, size, 2)
        for sample, first, _, size in spans(chunk)
    ]
    return jnp.concatenate(runs, axis=2)


def pack_kernel(chunk, slots, width, source, *rest):
    outs, sems = rest[:-1], rest[-1]
    me = lax.axis_index("seq")
    copies = []
    for out, slot in zip(outs, slots, strict=True):
        for sample, first, cols, size in spans(chunk):
            start = pl.multiple_of(lax.bitwise_xor(me, slot) * width + first, HD)
            part = source.at[:, 0, sample, :, pl.ds(start, size)]
            copies.append(pltpu.make_async_copy(part, out.at[:, :, cols], sems.at[len(copies)]))
    for copy in copies:
        copy.start()
    for copy in copies:
        copy.wait()


def pack(qkv, chunk, slots, width):
    shape = jax.ShapeDtypeStruct((3, qkv.shape[3], len(chunk) * HD), qkv.dtype)
    count = len(slots) * len(spans(chunk))
    return pl.pallas_call(
        functools.partial(pack_kernel, chunk, slots, width),
        out_shape=[shape] * len(slots),
        in_specs=[HBM],
        out_specs=[VMEM] * len(slots),
        scratch_shapes=[pltpu.SemaphoreType.DMA((count,))],
        compiler_params=pltpu.CompilerParams(vmem_limit_bytes=62 * 1024 * 1024),
        name="pack",
    )(qkv)


def normed(rows, gain, bias):
    grouped = rows.astype(jnp.float32)
    centred = grouped - jnp.mean(grouped, axis=-1, keepdims=True)
    spread = jnp.mean(centred * centred, axis=-1, keepdims=True)
    return (centred * lax.rsqrt(spread + 1e-06) * gain + bias).astype(jnp.bfloat16)


def attend_kernel(chunk, slots, width, fetch, layer, qkv, *rest):
    count = len(slots)
    half = count // 2
    landed, rest = dict(zip(slots[:-1], rest[: count - 1], strict=True)), rest[count - 1 :]
    held, sems = rest[-2:]
    outs = rest[-2 - count : -2]
    given = rest[: -2 - count]
    rows = held.shape[2]
    copies = []
    own = lax.axis_index("seq") * width
    for sample, first, cols, size in spans(chunk):
        start = pl.multiple_of(own + first, HD)
        part = qkv.at[:, 0, sample, :, pl.ds(start, size)]
        copies.append(pltpu.make_async_copy(part, held.at[0, :, :, cols], sems.at[len(copies)]))
    if fetch:
        for slot in range(1, count):
            copies.append(pltpu.make_async_copy(landed[slot], held.at[slot], sems.at[len(copies)]))
            landed[slot] = held.at[slot]
    landed[0] = held.at[0]
    for copy in copies:
        copy.start()
    done = 0
    for out, before in zip(outs, given):
        done = before.shape[1]
        out[:, :done] = before[...]
    if fetch:
        for copy in copies:
            copy.wait()
    for place, (_, head) in enumerate(chunk):
        cols = slice(place * HD, (place + 1) * HD)
        gains = layer[:, head * HD : (head + 1) * HD].astype(jnp.float32)
        others = [
            normed(landed[slot][1, :, cols], gains[2:3], gains[3:4]) for slot in range(1, count)
        ]
        if place == 0 and not fetch:
            for copy in copies:
                copy.wait()
        keys = jnp.concatenate([normed(landed[0][1, :, cols], gains[2:3], gains[3:4])] + others)
        values = jnp.concatenate([landed[slot][2, :, cols] for slot in range(count)])
        per_block = max(1, 512 // rows)
        for first in range(0, count, per_block):
            here = range(first, min(first + per_block, count))
            queries = jnp.concatenate(
                [normed(landed[slot][0, :, cols], gains[0:1], gains[1:2]) for slot in here]
            )
            scores = lax.dot_general(
                queries, keys, (((1,), (1,)), ((), ())), preferred_element_type=jnp.float32
            )
            top = jnp.max(scores, axis=-1, keepdims=True)
            raised = jnp.exp2((scores - top) * (HD**-0.5 * LOG2E))
            total = jnp.sum(raised, axis=-1, keepdims=True)
            probs = (raised * (1.0 / total)).astype(jnp.bfloat16)
            result = jnp.dot(probs, values, preferred_element_type=jnp.float32)
            result = result.astype(jnp.bfloat16)
            for turn, slot in enumerate(here):
                part = result[turn * rows : (turn + 1) * rows]
                if slot < half:
                    outs[slot][:, done + place * HD : done + (place + 1) * HD] = part
                else:
                    outs[slot][:, cols] = part


def attend(chunk, slots, width, fetch, layer, qkv, arrived, given):
    count = len(slots)
    half = count // 2
    _, rows, cols = arrived[0].shape
    patches = count * rows
    before = given[0].shape[1] if given else 0
    outs = pl.pallas_call(
        functools.partial(attend_kernel, chunk, slots, width, fetch),
        out_shape=[jax.ShapeDtypeStruct((rows, before + cols), jnp.bfloat16)] * half
        + [jax.ShapeDtypeStruct((rows, cols), jnp.bfloat16)] * half,
        in_specs=[VMEM, HBM]
        + [ANY if fetch else VMEM] * (count - 1)
        + [VMEM] * len(given),
        out_specs=[VMEM] * count,
        scratch_shapes=[
            pltpu.VMEM((count if fetch else 1, 3, rows, cols), jnp.bfloat16),
            pltpu.SemaphoreType.DMA((len(spans(chunk)) + count,)),
        ],
        compiler_params=pltpu.CompilerParams(vmem_limit_bytes=16 * 1024 * 1024),
        cost_estimate=pl.CostEstimate(
            flops=4 * patches * patches * cols,
            bytes_accessed=8 * patches * cols,
            transcendentals=patches * patches * len(chunk),
        ),
        name="attend",
    )(layer, qkv, *arrived, *given)
    return list(outs[:half]), list(outs[half:])


def unpack_kernel(places, width, *rest):
    parts, out, sems = rest[: len(places)], rest[-2], rest[-1]
    me = lax.axis_index("seq")
    copies = []
    for part, (chunk, slot) in zip(parts, places, strict=True):
        for sample, first, cols, size in spans(chunk):
            start = pl.multiple_of(lax.bitwise_xor(me, slot) * width + first, HD)
            there = out.at[0, sample, :, pl.ds(start, size)]
            copies.append(pltpu.make_async_copy(part.at[:, cols], there, sems.at[len(copies)]))
    for copy in copies:
        copy.start()
    for copy in copies:
        copy.wait()


def unpack(parts, places, width, shape):
    return pl.pallas_call(
        functools.partial(unpack_kernel, places, width),
        out_shape=jax.ShapeDtypeStruct(shape, parts[0].dtype),
        in_specs=[VMEM] * len(parts),
        out_specs=ANY,
        scratch_shapes=[
            pltpu.SemaphoreType.DMA((sum(len(spans(chunk)) for chunk, _ in places),))
        ],
        compiler_params=pltpu.CompilerParams(vmem_limit_bytes=4 * 1024 * 1024),
        name="unpack",
    )(*parts)


def swap(part, slot):
    if slot == 0:
        return part
    return lax.ppermute(part, "seq", [(place, place ^ slot) for place in range(lax.axis_size("seq"))])


def mixed(one, other):
    return [slot for pair in zip(one, other, strict=True) for slot in pair]


def shards(dp_count, seq_count, qkv, master, moment_one, moment_two, grads):
    width = qkv.shape[4] // seq_count
    half = seq_count // 2
    far, near = list(range(half, seq_count)), list(range(1, half))
    turned = far[half // 2 :] + far[: half // 2]
    pairs = [(sample, head) for sample in range(qkv.shape[2]) for head in range(width // HD)]
    cut = len(pairs) - max(1, len(pairs) // 2)
    chunks = [pairs[:cut], pairs[cut:]]
    orders = [
        [turned[0], near[0], turned[1]] + mixed(turned[2:], near[1:]) + [0],
        mixed(far, near + [0]),
    ]
    landed = []
    for chunk, slots in zip(chunks, orders, strict=True):
        parts = [] if landed else [cut_out(qkv, chunk, slots[0], width)]
        parts += pack(qkv, chunk, slots[len(parts) : -1], width)
        landed.append([swap(part, slot) for part, slot in zip(parts, slots[:-1], strict=True)])
    updated, first_moment, second_moment = adamw(master, moment_one, moment_two, grads)
    layer = own_columns(updated.astype(jnp.bfloat16), dp_count, seq_count, width)
    parts, places, near_out = [], [], []
    for turn, (chunk, slots) in enumerate(zip(chunks, orders, strict=True)):
        near_out, far_out = attend(
            chunk, slots, width, turn == 0, layer, qkv, landed[turn], near_out
        )
        parts += [swap(out, slot) for out, slot in zip(far_out, far, strict=True)]
        places += [(chunk, slot) for slot in far]
    for slot in near[1:] + near[:1] + [0]:
        parts.append(swap(near_out[slot], slot))
        places.append((pairs, slot))
    attended = unpack(parts, places, width, (1, *qkv.shape[2:]))
    return (attended, updated, first_moment, second_moment)


def solution(mesh):
    placed = (
        P(None, "dp", None, "seq", None),
        P(None, "dp"),
        P(None, "dp"),
        P(None, "dp"),
        P(None, "dp"),
    )
    return jax.shard_map(
        functools.partial(shards, mesh.shape["dp"], mesh.shape["seq"]),
        mesh=mesh,
        in_specs=placed,
        out_specs=(P("dp", None, "seq", None), P(None, "dp"), P(None, "dp"), P(None, "dp")),
        check_vma=False,
    )
```

```python
import functools

import jax
import jax.numpy as jnp
from jax import lax
from jax.experimental import pallas as pl
from jax.experimental.pallas import tpu as pltpu
from jax.sharding import PartitionSpec as P

HEADS = 32
HD = 128
OPT_STEP = 10

BETA_ONE = 0.9
BETA_TWO = 0.95
RATE = 0.02
DECAY = 0.1
EPSILON = 1e-08

LOG2E = 1.4426950408889634
ANY = pl.BlockSpec(memory_space=pl.ANY)
HBM = pl.BlockSpec(memory_space=pltpu.HBM)
VMEM = pl.BlockSpec(memory_space=pltpu.VMEM)


def adamw(master, moment_one, moment_two, grads):
    first_moment = BETA_ONE * moment_one + (1.0 - BETA_ONE) * grads
    second_moment = BETA_TWO * moment_two + (1.0 - BETA_TWO) * grads * grads
    first_hat = first_moment / (1.0 - BETA_ONE**OPT_STEP)
    second_hat = second_moment / (1.0 - BETA_TWO**OPT_STEP)
    updated = master - RATE * (first_hat / (jnp.sqrt(second_hat) + EPSILON) + DECAY * master)
    return (updated, first_moment, second_moment)


def own_columns(layer, dp_count, seq_count, width):
    shard_cols = layer.shape[1]
    assert shard_cols % width == 0
    rounds = [[] for _ in range(dp_count - 1)]
    for seq in range(seq_count):
        owner = seq * width // shard_cols
        for turn, pairs in enumerate(rounds):
            other = (owner + turn + 1) % dp_count
            pairs.append((owner * seq_count + seq, other * seq_count + seq))
    first_col = lax.axis_index("seq") * width
    mine = lax.axis_index("dp") == first_col // shard_cols
    found = jnp.where(mine, layer, jnp.zeros_like(layer))
    for pairs in rounds:
        found = found + lax.ppermute(layer, ("dp", "seq"), pairs)
    return lax.dynamic_slice_in_dim(found, first_col % shard_cols, width, 1)


def spans(chunk):
    runs = []
    for place, (sample, head) in enumerate(chunk):
        if runs and runs[-1][0] == sample and runs[-1][1] + runs[-1][2] == head:
            runs[-1][2] += 1
        else:
            runs.append([sample, head, 1, place])
    return [
        (sample, first * HD, slice(place * HD, (place + count) * HD), count * HD)
        for sample, first, count, place in runs
    ]


def cut_out(qkv, chunk, slot, width):
    own = lax.bitwise_xor(lax.axis_index("seq"), slot) * width
    runs = [
        lax.dynamic_slice_in_dim(qkv[:, 0, sample], own + first, size, 2)
        for sample, first, _, size in spans(chunk)
    ]
    return jnp.concatenate(runs, axis=2)


def pack_kernel(chunk, slots, width, source, *rest):
    outs, sems = rest[:-1], rest[-1]
    me = lax.axis_index("seq")
    copies = []
    for out, slot in zip(outs, slots, strict=True):
        for sample, first, cols, size in spans(chunk):
            start = pl.multiple_of(lax.bitwise_xor(me, slot) * width + first, HD)
            part = source.at[:, 0, sample, :, pl.ds(start, size)]
            copies.append(pltpu.make_async_copy(part, out.at[:, :, cols], sems.at[len(copies)]))
    for copy in copies:
        copy.start()
    for copy in copies:
        copy.wait()


def pack(qkv, chunk, slots, width):
    shape = jax.ShapeDtypeStruct((3, qkv.shape[3], len(chunk) * HD), qkv.dtype)
    count = len(slots) * len(spans(chunk))
    return pl.pallas_call(
        functools.partial(pack_kernel, chunk, slots, width),
        out_shape=[shape] * len(slots),
        in_specs=[HBM],
        out_specs=[VMEM] * len(slots),
        scratch_shapes=[pltpu.SemaphoreType.DMA((count,))],
        compiler_params=pltpu.CompilerParams(vmem_limit_bytes=62 * 1024 * 1024),
        name="pack",
    )(qkv)


def normed(rows, gain, bias):
    grouped = rows.astype(jnp.float32)
    centred = grouped - jnp.mean(grouped, axis=-1, keepdims=True)
    spread = jnp.mean(centred * centred, axis=-1, keepdims=True)
    return (centred * lax.rsqrt(spread + 1e-06) * gain + bias).astype(jnp.bfloat16)


def attend_kernel(chunk, slots, joined, width, fetch, layer, qkv, *rest):
    count = len(slots)
    landed, rest = dict(zip(slots[:-1], rest[: count - 1], strict=True)), rest[count - 1 :]
    held, sems = rest[-2:]
    outs = rest[-2 - count : -2]
    given = rest[: -2 - count]
    rows = held.shape[2]
    copies = []
    own = lax.axis_index("seq") * width
    for sample, first, cols, size in spans(chunk):
        start = pl.multiple_of(own + first, HD)
        part = qkv.at[:, 0, sample, :, pl.ds(start, size)]
        copies.append(pltpu.make_async_copy(part, held.at[0, :, :, cols], sems.at[len(copies)]))
    if fetch:
        for slot in range(1, count):
            copies.append(pltpu.make_async_copy(landed[slot], held.at[slot], sems.at[len(copies)]))
            landed[slot] = held.at[slot]
    landed[0] = held.at[0]
    for copy in copies:
        copy.start()
    done = [0] * count
    for slot, before in zip(joined, given):
        done[slot] = before.shape[1]
        outs[slot][:, : done[slot]] = before[...]
    if fetch:
        for copy in copies:
            copy.wait()
    for place, (_, head) in enumerate(chunk):
        cols = slice(place * HD, (place + 1) * HD)
        gains = layer[:, head * HD : (head + 1) * HD].astype(jnp.float32)
        others = [
            normed(landed[slot][1, :, cols], gains[2:3], gains[3:4]) for slot in range(1, count)
        ]
        if place == 0 and not fetch:
            for copy in copies:
                copy.wait()
        keys = jnp.concatenate([normed(landed[0][1, :, cols], gains[2:3], gains[3:4])] + others)
        values = jnp.concatenate([landed[slot][2, :, cols] for slot in range(count)])
        per_block = max(1, 512 // rows)
        for first in range(0, count, per_block):
            here = range(first, min(first + per_block, count))
            queries = jnp.concatenate(
                [normed(landed[slot][0, :, cols], gains[0:1], gains[1:2]) for slot in here]
            )
            scores = lax.dot_general(
                queries, keys, (((1,), (1,)), ((), ())), preferred_element_type=jnp.float32
            )
            top = jnp.max(scores, axis=-1, keepdims=True)
            raised = jnp.exp2((scores - top) * (HD**-0.5 * LOG2E))
            total = jnp.sum(raised, axis=-1, keepdims=True)
            probs = (raised * (1.0 / total)).astype(jnp.bfloat16)
            result = jnp.dot(probs, values, preferred_element_type=jnp.float32)
            result = result.astype(jnp.bfloat16)
            for turn, slot in enumerate(here):
                part = result[turn * rows : (turn + 1) * rows]
                start = done[slot] + place * HD
                outs[slot][:, start : start + HD] = part


def attend(chunk, slots, joined, width, fetch, layer, qkv, arrived, given):
    count = len(slots)
    _, rows, cols = arrived[0].shape
    patches = count * rows
    before = given[0].shape[1] if given else 0
    outs = pl.pallas_call(
        functools.partial(attend_kernel, chunk, slots, joined, width, fetch),
        out_shape=[
            jax.ShapeDtypeStruct((rows, cols + (before if slot in joined else 0)), jnp.bfloat16)
            for slot in range(count)
        ],
        in_specs=[VMEM, HBM]
        + [ANY if fetch else VMEM] * (count - 1)
        + [VMEM] * len(given),
        out_specs=[VMEM] * count,
        scratch_shapes=[
            pltpu.VMEM((count if fetch else 1, 3, rows, cols), jnp.bfloat16),
            pltpu.SemaphoreType.DMA((len(spans(chunk)) + count,)),
        ],
        compiler_params=pltpu.CompilerParams(vmem_limit_bytes=16 * 1024 * 1024),
        cost_estimate=pl.CostEstimate(
            flops=4 * patches * patches * cols,
            bytes_accessed=8 * patches * cols,
            transcendentals=patches * patches * len(chunk),
        ),
        name="attend",
    )(layer, qkv, *arrived, *given)
    return list(outs)


def unpack_kernel(places, width, *rest):
    parts, out, sems = rest[: len(places)], rest[-2], rest[-1]
    me = lax.axis_index("seq")
    copies = []
    for part, (chunk, slot) in zip(parts, places, strict=True):
        for sample, first, cols, size in spans(chunk):
            start = pl.multiple_of(lax.bitwise_xor(me, slot) * width + first, HD)
            there = out.at[0, sample, :, pl.ds(start, size)]
            copies.append(pltpu.make_async_copy(part.at[:, cols], there, sems.at[len(copies)]))
    for copy in copies:
        copy.start()
    for copy in copies:
        copy.wait()


def unpack(parts, places, width, shape):
    return pl.pallas_call(
        functools.partial(unpack_kernel, places, width),
        out_shape=jax.ShapeDtypeStruct(shape, parts[0].dtype),
        in_specs=[VMEM] * len(parts),
        out_specs=ANY,
        scratch_shapes=[
            pltpu.SemaphoreType.DMA((sum(len(spans(chunk)) for chunk, _ in places),))
        ],
        compiler_params=pltpu.CompilerParams(vmem_limit_bytes=4 * 1024 * 1024),
        name="unpack",
    )(*parts)


def swap(part, slot):
    if slot == 0:
        return part
    return lax.ppermute(part, "seq", [(place, place ^ slot) for place in range(lax.axis_size("seq"))])


def mixed(one, other):
    return [slot for pair in zip(one, other, strict=True) for slot in pair]


def shards(dp_count, seq_count, qkv, master, moment_one, moment_two, grads):
    width = qkv.shape[4] // seq_count
    half = seq_count // 2
    far, near = list(range(half, seq_count)), list(range(1, half))
    turned = far[half // 2 :] + far[: half // 2]
    pairs = [(sample, head) for sample in range(qkv.shape[2]) for head in range(width // HD)]
    cut = len(pairs) - max(1, len(pairs) // 2)
    chunks = [pairs[:cut], pairs[cut:]]
    orders = [
        [turned[0], near[0], turned[1]] + mixed(turned[2:], near[1:]) + [0],
        mixed(far, near + [0]),
    ]
    landed = []
    for chunk, slots in zip(chunks, orders, strict=True):
        parts = [] if landed else [cut_out(qkv, chunk, slots[0], width)]
        parts += pack(qkv, chunk, slots[len(parts) : -1], width)
        landed.append([swap(part, slot) for part, slot in zip(parts, slots[:-1], strict=True)])
    updated, first_moment, second_moment = adamw(master, moment_one, moment_two, grads)
    layer = own_columns(updated.astype(jnp.bfloat16), dp_count, seq_count, width)
    joined, alone = [0] + near[:-1], near[-1]
    made, outs = {}, []
    for turn, (chunk, slots) in enumerate(zip(chunks, orders, strict=True)):
        given = [outs[slot] for slot in joined] if outs else []
        outs = attend(chunk, slots, joined, width, turn == 0, layer, qkv, landed[turn], given)
        made.update({(turn, slot): (out, chunk) for slot, out in enumerate(outs)})
    made.update({(1, slot): (outs[slot], pairs) for slot in joined})
    order = [(0, alone)] + [(turn, slot) for turn in range(2) for slot in far]
    order += [(1, slot) for slot in near[1:] + near[:1] + [0]]
    parts = [swap(made[key][0], key[1]) for key in order]
    places = [(made[key][1], key[1]) for key in order]
    attended = unpack(parts, places, width, (1, *qkv.shape[2:]))
    return (attended, updated, first_moment, second_moment)


def solution(mesh):
    placed = (
        P(None, "dp", None, "seq", None),
        P(None, "dp"),
        P(None, "dp"),
        P(None, "dp"),
        P(None, "dp"),
    )
    return jax.shard_map(
        functools.partial(shards, mesh.shape["dp"], mesh.shape["seq"]),
        mesh=mesh,
        in_specs=placed,
        out_specs=(P("dp", None, "seq", None), P(None, "dp"), P(None, "dp"), P(None, "dp")),
        check_vma=False,
    )
```

```python
import functools

import jax
import jax.numpy as jnp
from jax import lax
from jax.experimental import pallas as pl
from jax.experimental.pallas import tpu as pltpu
from jax.sharding import PartitionSpec as P

HEADS = 32
HD = 128
OPT_STEP = 10

BETA_ONE = 0.9
BETA_TWO = 0.95
RATE = 0.02
DECAY = 0.1
EPSILON = 1e-08

LOG2E = 1.4426950408889634
ANY = pl.BlockSpec(memory_space=pl.ANY)
HBM = pl.BlockSpec(memory_space=pltpu.HBM)
VMEM = pl.BlockSpec(memory_space=pltpu.VMEM)


def adamw(master, moment_one, moment_two, grads):
    first_moment = BETA_ONE * moment_one + (1.0 - BETA_ONE) * grads
    second_moment = BETA_TWO * moment_two + (1.0 - BETA_TWO) * grads * grads
    first_hat = first_moment / (1.0 - BETA_ONE**OPT_STEP)
    second_hat = second_moment / (1.0 - BETA_TWO**OPT_STEP)
    updated = master - RATE * (first_hat / (jnp.sqrt(second_hat) + EPSILON) + DECAY * master)
    return (updated, first_moment, second_moment)


def own_columns(layer, dp_count, seq_count, width):
    shard_cols = layer.shape[1]
    assert shard_cols % width == 0
    rounds = [[] for _ in range(dp_count - 1)]
    for seq in range(seq_count):
        owner = seq * width // shard_cols
        for turn, pairs in enumerate(rounds):
            other = (owner + turn + 1) % dp_count
            pairs.append((owner * seq_count + seq, other * seq_count + seq))
    first_col = lax.axis_index("seq") * width
    mine = lax.axis_index("dp") == first_col // shard_cols
    found = jnp.where(mine, layer, jnp.zeros_like(layer))
    for pairs in rounds:
        found = found + lax.ppermute(layer, ("dp", "seq"), pairs)
    return lax.dynamic_slice_in_dim(found, first_col % shard_cols, width, 1)


def spans(chunk):
    runs = []
    for place, (sample, head) in enumerate(chunk):
        if runs and runs[-1][0] == sample and runs[-1][1] + runs[-1][2] == head:
            runs[-1][2] += 1
        else:
            runs.append([sample, head, 1, place])
    return [
        (sample, first * HD, slice(place * HD, (place + count) * HD), count * HD)
        for sample, first, count, place in runs
    ]


def cut_out(qkv, chunk, slot, width):
    own = lax.bitwise_xor(lax.axis_index("seq"), slot) * width
    runs = [
        lax.dynamic_slice_in_dim(qkv[:, 0, sample], own + first, size, 2)
        for sample, first, _, size in spans(chunk)
    ]
    return jnp.concatenate(runs, axis=2)


def pack_kernel(chunk, slots, width, source, *rest):
    outs, sems = rest[:-1], rest[-1]
    me = lax.axis_index("seq")
    copies = []
    for out, slot in zip(outs, slots, strict=True):
        for sample, first, cols, size in spans(chunk):
            start = pl.multiple_of(lax.bitwise_xor(me, slot) * width + first, HD)
            for which in range(3):
                part = source.at[which, 0, sample, :, pl.ds(start, size)]
                there = out.at[which, :, cols]
                copies.append(pltpu.make_async_copy(part, there, sems.at[len(copies)]))
    for copy in copies:
        copy.start()
    for copy in copies:
        copy.wait()


def pack(qkv, chunk, slots, width):
    shape = jax.ShapeDtypeStruct((3, qkv.shape[3], len(chunk) * HD), qkv.dtype)
    count = 3 * len(slots) * len(spans(chunk))
    return pl.pallas_call(
        functools.partial(pack_kernel, chunk, slots, width),
        out_shape=[shape] * len(slots),
        in_specs=[HBM],
        out_specs=[VMEM] * len(slots),
        scratch_shapes=[pltpu.SemaphoreType.DMA((count,))],
        compiler_params=pltpu.CompilerParams(vmem_limit_bytes=62 * 1024 * 1024),
        name="pack",
    )(qkv)


def normed(rows, gain, bias):
    grouped = rows.astype(jnp.float32)
    centred = grouped - jnp.mean(grouped, axis=-1, keepdims=True)
    spread = jnp.mean(centred * centred, axis=-1, keepdims=True)
    return (centred * lax.rsqrt(spread + 1e-06) * gain + bias).astype(jnp.bfloat16)


def attend_kernel(chunk, slots, joined, width, fetch, layer, qkv, *rest):
    count = len(slots)
    landed, rest = dict(zip(slots[:-1], rest[: count - 1], strict=True)), rest[count - 1 :]
    held, sems = rest[-2:]
    outs = rest[-2 - count : -2]
    given = rest[: -2 - count]
    rows = held.shape[2]
    copies = []
    own = lax.axis_index("seq") * width
    for sample, first, cols, size in spans(chunk):
        start = pl.multiple_of(own + first, HD)
        part = qkv.at[:, 0, sample, :, pl.ds(start, size)]
        copies.append(pltpu.make_async_copy(part, held.at[0, :, :, cols], sems.at[len(copies)]))
    if fetch:
        for slot in range(1, count):
            copies.append(pltpu.make_async_copy(landed[slot], held.at[slot], sems.at[len(copies)]))
            landed[slot] = held.at[slot]
    landed[0] = held.at[0]
    for copy in copies:
        copy.start()
    done = [0] * count
    for slot, before in zip(joined, given):
        done[slot] = before.shape[1]
        outs[slot][:, : done[slot]] = before[...]
    if fetch:
        for copy in copies:
            copy.wait()
    for place, (_, head) in enumerate(chunk):
        cols = slice(place * HD, (place + 1) * HD)
        gains = layer[:, head * HD : (head + 1) * HD].astype(jnp.float32)
        others = [
            normed(landed[slot][1, :, cols], gains[2:3], gains[3:4]) for slot in range(1, count)
        ]
        if place == 0 and not fetch:
            for copy in copies:
                copy.wait()
        keys = jnp.concatenate([normed(landed[0][1, :, cols], gains[2:3], gains[3:4])] + others)
        values = jnp.concatenate([landed[slot][2, :, cols] for slot in range(count)])
        per_block = max(1, 512 // rows)
        for first in range(0, count, per_block):
            here = range(first, min(first + per_block, count))
            queries = jnp.concatenate(
                [normed(landed[slot][0, :, cols], gains[0:1], gains[1:2]) for slot in here]
            )
            scores = lax.dot_general(
                queries, keys, (((1,), (1,)), ((), ())), preferred_element_type=jnp.float32
            )
            top = jnp.max(scores, axis=-1, keepdims=True)
            raised = jnp.exp2((scores - top) * (HD**-0.5 * LOG2E))
            total = jnp.sum(raised, axis=-1, keepdims=True)
            probs = (raised * (1.0 / total)).astype(jnp.bfloat16)
            result = jnp.dot(probs, values, preferred_element_type=jnp.float32)
            result = result.astype(jnp.bfloat16)
            for turn, slot in enumerate(here):
                part = result[turn * rows : (turn + 1) * rows]
                start = done[slot] + place * HD
                outs[slot][:, start : start + HD] = part


def attend(chunk, slots, joined, width, fetch, layer, qkv, arrived, given):
    count = len(slots)
    _, rows, cols = arrived[0].shape
    patches = count * rows
    before = given[0].shape[1] if given else 0
    outs = pl.pallas_call(
        functools.partial(attend_kernel, chunk, slots, joined, width, fetch),
        out_shape=[
            jax.ShapeDtypeStruct((rows, cols + (before if slot in joined else 0)), jnp.bfloat16)
            for slot in range(count)
        ],
        in_specs=[VMEM, HBM]
        + [ANY if fetch else VMEM] * (count - 1)
        + [VMEM] * len(given),
        out_specs=[VMEM] * count,
        scratch_shapes=[
            pltpu.VMEM((count if fetch else 1, 3, rows, cols), jnp.bfloat16),
            pltpu.SemaphoreType.DMA((len(spans(chunk)) + count,)),
        ],
        compiler_params=pltpu.CompilerParams(vmem_limit_bytes=16 * 1024 * 1024),
        cost_estimate=pl.CostEstimate(
            flops=4 * patches * patches * cols,
            bytes_accessed=8 * patches * cols,
            transcendentals=patches * patches * len(chunk),
        ),
        name="attend",
    )(layer, qkv, *arrived, *given)
    return list(outs)


def unpack_kernel(places, width, *rest):
    parts, out, sems = rest[: len(places)], rest[-2], rest[-1]
    me = lax.axis_index("seq")
    copies = []
    for part, (chunk, slot) in zip(parts, places, strict=True):
        for sample, first, cols, size in spans(chunk):
            start = pl.multiple_of(lax.bitwise_xor(me, slot) * width + first, HD)
            there = out.at[0, sample, :, pl.ds(start, size)]
            copies.append(pltpu.make_async_copy(part.at[:, cols], there, sems.at[len(copies)]))
    for copy in copies:
        copy.start()
    for copy in copies:
        copy.wait()


def unpack(parts, places, width, shape):
    return pl.pallas_call(
        functools.partial(unpack_kernel, places, width),
        out_shape=jax.ShapeDtypeStruct(shape, parts[0].dtype),
        in_specs=[VMEM] * len(parts),
        out_specs=ANY,
        scratch_shapes=[
            pltpu.SemaphoreType.DMA((sum(len(spans(chunk)) for chunk, _ in places),))
        ],
        compiler_params=pltpu.CompilerParams(vmem_limit_bytes=4 * 1024 * 1024),
        name="unpack",
    )(*parts)


def swap(part, slot):
    if slot == 0:
        return part
    return lax.ppermute(part, "seq", [(place, place ^ slot) for place in range(lax.axis_size("seq"))])


def mixed(one, other):
    return [slot for pair in zip(one, other, strict=True) for slot in pair]


def shards(dp_count, seq_count, qkv, master, moment_one, moment_two, grads):
    width = qkv.shape[4] // seq_count
    half = seq_count // 2
    far, near = list(range(half, seq_count)), list(range(1, half))
    turned = far[half // 2 :] + far[: half // 2]
    pairs = [(sample, head) for sample in range(qkv.shape[2]) for head in range(width // HD)]
    cut = len(pairs) - max(1, len(pairs) // 2)
    chunks = [pairs[:cut], pairs[cut:]]
    orders = [
        [turned[0], near[0], turned[1]] + mixed(turned[2:], near[1:]) + [0],
        mixed(far, near + [0]),
    ]
    landed = []
    for chunk, slots in zip(chunks, orders, strict=True):
        parts = [] if landed else [cut_out(qkv, chunk, slots[0], width)]
        parts += pack(qkv, chunk, slots[len(parts) : -1], width)
        landed.append([swap(part, slot) for part, slot in zip(parts, slots[:-1], strict=True)])
    updated, first_moment, second_moment = adamw(master, moment_one, moment_two, grads)
    layer = own_columns(updated.astype(jnp.bfloat16), dp_count, seq_count, width)
    joined, alone = [0] + near[:-1], near[-1]
    made, outs = {}, []
    for turn, (chunk, slots) in enumerate(zip(chunks, orders, strict=True)):
        given = [outs[slot] for slot in joined] if outs else []
        outs = attend(chunk, slots, joined, width, turn == 0, layer, qkv, landed[turn], given)
        made.update({(turn, slot): (out, chunk) for slot, out in enumerate(outs)})
    made.update({(1, slot): (outs[slot], pairs) for slot in joined})
    order = [(0, alone)] + [(turn, slot) for turn in range(2) for slot in far]
    order += [(1, slot) for slot in near[1:] + near[:1] + [0]]
    parts = [swap(made[key][0], key[1]) for key in order]
    places = [(made[key][1], key[1]) for key in order]
    attended = unpack(parts, places, width, (1, *qkv.shape[2:]))
    return (attended, updated, first_moment, second_moment)


def solution(mesh):
    placed = (
        P(None, "dp", None, "seq", None),
        P(None, "dp"),
        P(None, "dp"),
        P(None, "dp"),
        P(None, "dp"),
    )
    return jax.shard_map(
        functools.partial(shards, mesh.shape["dp"], mesh.shape["seq"]),
        mesh=mesh,
        in_specs=placed,
        out_specs=(P("dp", None, "seq", None), P(None, "dp"), P(None, "dp"), P(None, "dp")),
        check_vma=False,
    )
```

```python
import functools

import jax
import jax.numpy as jnp
from jax import lax
from jax.experimental import pallas as pl
from jax.experimental.pallas import tpu as pltpu
from jax.sharding import PartitionSpec as P

HEADS = 32
HD = 128
OPT_STEP = 10

BETA_ONE = 0.9
BETA_TWO = 0.95
RATE = 0.02
DECAY = 0.1
EPSILON = 1e-08

LOG2E = 1.4426950408889634
ANY = pl.BlockSpec(memory_space=pl.ANY)
HBM = pl.BlockSpec(memory_space=pltpu.HBM)
VMEM = pl.BlockSpec(memory_space=pltpu.VMEM)


def adamw(master, moment_one, moment_two, grads):
    first_moment = BETA_ONE * moment_one + (1.0 - BETA_ONE) * grads
    second_moment = BETA_TWO * moment_two + (1.0 - BETA_TWO) * grads * grads
    first_hat = first_moment / (1.0 - BETA_ONE**OPT_STEP)
    second_hat = second_moment / (1.0 - BETA_TWO**OPT_STEP)
    updated = master - RATE * (first_hat / (jnp.sqrt(second_hat) + EPSILON) + DECAY * master)
    return (updated, first_moment, second_moment)


def own_columns(layer, dp_count, seq_count, width):
    shard_cols = layer.shape[1]
    assert shard_cols % width == 0
    rounds = [[] for _ in range(dp_count - 1)]
    for seq in range(seq_count):
        owner = seq * width // shard_cols
        for turn, pairs in enumerate(rounds):
            other = (owner + turn + 1) % dp_count
            pairs.append((owner * seq_count + seq, other * seq_count + seq))
    first_col = lax.axis_index("seq") * width
    mine = lax.axis_index("dp") == first_col // shard_cols
    found = jnp.where(mine, layer, jnp.zeros_like(layer))
    for pairs in rounds:
        found = found + lax.ppermute(layer, ("dp", "seq"), pairs)
    return lax.dynamic_slice_in_dim(found, first_col % shard_cols, width, 1)


def spans(chunk):
    runs = []
    for place, (sample, head) in enumerate(chunk):
        if runs and runs[-1][0] == sample and runs[-1][1] + runs[-1][2] == head:
            runs[-1][2] += 1
        else:
            runs.append([sample, head, 1, place])
    return [
        (sample, first * HD, slice(place * HD, (place + count) * HD), count * HD)
        for sample, first, count, place in runs
    ]


def cut_out(qkv, chunk, slot, width):
    own = lax.bitwise_xor(lax.axis_index("seq"), slot) * width
    runs = [
        lax.dynamic_slice_in_dim(qkv[:, 0, sample], own + first, size, 2)
        for sample, first, _, size in spans(chunk)
    ]
    return jnp.concatenate(runs, axis=2)


def pack_kernel(chunk, slots, width, source, *rest):
    outs, sems = rest[:-1], rest[-1]
    me = lax.axis_index("seq")
    copies = []
    for out, slot in zip(outs, slots, strict=True):
        for sample, first, cols, size in spans(chunk):
            start = pl.multiple_of(lax.bitwise_xor(me, slot) * width + first, HD)
            for which in range(3):
                part = source.at[which, 0, sample, :, pl.ds(start, size)]
                there = out.at[which, :, cols]
                copies.append(pltpu.make_async_copy(part, there, sems.at[len(copies)]))
    for copy in copies:
        copy.start()
    for copy in copies:
        copy.wait()


def pack(qkv, chunk, slots, width):
    shape = jax.ShapeDtypeStruct((3, qkv.shape[3], len(chunk) * HD), qkv.dtype)
    count = 3 * len(slots) * len(spans(chunk))
    return pl.pallas_call(
        functools.partial(pack_kernel, chunk, slots, width),
        out_shape=[shape] * len(slots),
        in_specs=[HBM],
        out_specs=[VMEM] * len(slots),
        scratch_shapes=[pltpu.SemaphoreType.DMA((count,))],
        compiler_params=pltpu.CompilerParams(vmem_limit_bytes=62 * 1024 * 1024),
        name="pack",
    )(qkv)


def normed(rows, gain, bias):
    grouped = rows.astype(jnp.float32)
    centred = grouped - jnp.mean(grouped, axis=-1, keepdims=True)
    spread = jnp.mean(centred * centred, axis=-1, keepdims=True)
    return (centred * lax.rsqrt(spread + 1e-06) * gain + bias).astype(jnp.bfloat16)


def attend_kernel(chunk, slots, joined, width, fetch, layer, qkv, *rest):
    count = len(slots)
    landed, rest = dict(zip(slots[:-1], rest[: count - 1], strict=True)), rest[count - 1 :]
    held, sems = rest[-2:]
    outs = rest[-2 - count : -2]
    given = rest[: -2 - count]
    rows = held.shape[2]
    copies = []
    own = lax.axis_index("seq") * width
    for sample, first, cols, size in spans(chunk):
        start = pl.multiple_of(own + first, HD)
        part = qkv.at[:, 0, sample, :, pl.ds(start, size)]
        copies.append(pltpu.make_async_copy(part, held.at[0, :, :, cols], sems.at[len(copies)]))
    if fetch:
        for slot in range(1, count):
            copies.append(pltpu.make_async_copy(landed[slot], held.at[slot], sems.at[len(copies)]))
            landed[slot] = held.at[slot]
    landed[0] = held.at[0]
    for copy in copies:
        copy.start()
    done = [0] * count
    for slot, before in zip(joined, given):
        done[slot] = before.shape[1]
        outs[slot][:, : done[slot]] = before[...]
    if fetch:
        for copy in copies:
            copy.wait()
    for place, (_, head) in enumerate(chunk):
        cols = slice(place * HD, (place + 1) * HD)
        gains = layer[:, head * HD : (head + 1) * HD].astype(jnp.float32)
        others = [
            normed(landed[slot][1, :, cols], gains[2:3], gains[3:4]) for slot in range(1, count)
        ]
        if place == 0 and not fetch:
            for copy in copies:
                copy.wait()
        keys = jnp.concatenate([normed(landed[0][1, :, cols], gains[2:3], gains[3:4])] + others)
        values = jnp.concatenate([landed[slot][2, :, cols] for slot in range(count)])
        per_block = max(1, 512 // rows)
        for first in range(0, count, per_block):
            here = range(first, min(first + per_block, count))
            queries = jnp.concatenate(
                [normed(landed[slot][0, :, cols], gains[0:1], gains[1:2]) for slot in here]
            )
            scores = lax.dot_general(
                queries, keys, (((1,), (1,)), ((), ())), preferred_element_type=jnp.float32
            )
            top = jnp.max(scores, axis=-1, keepdims=True)
            raised = jnp.exp2((scores - top) * (HD**-0.5 * LOG2E))
            total = jnp.sum(raised, axis=-1, keepdims=True)
            probs = (raised * (1.0 / total)).astype(jnp.bfloat16)
            result = jnp.dot(probs, values, preferred_element_type=jnp.float32)
            result = result.astype(jnp.bfloat16)
            for turn, slot in enumerate(here):
                part = result[turn * rows : (turn + 1) * rows]
                start = done[slot] + place * HD
                outs[slot][:, start : start + HD] = part


def attend(chunk, slots, joined, width, fetch, layer, qkv, arrived, given):
    count = len(slots)
    _, rows, cols = arrived[0].shape
    patches = count * rows
    before = given[0].shape[1] if given else 0
    outs = pl.pallas_call(
        functools.partial(attend_kernel, chunk, slots, joined, width, fetch),
        out_shape=[
            jax.ShapeDtypeStruct((rows, cols + (before if slot in joined else 0)), jnp.bfloat16)
            for slot in range(count)
        ],
        in_specs=[VMEM, HBM]
        + [ANY if fetch else VMEM] * (count - 1)
        + [VMEM] * len(given),
        out_specs=[VMEM] * count,
        scratch_shapes=[
            pltpu.VMEM((count if fetch else 1, 3, rows, cols), jnp.bfloat16),
            pltpu.SemaphoreType.DMA((len(spans(chunk)) + count,)),
        ],
        compiler_params=pltpu.CompilerParams(vmem_limit_bytes=16 * 1024 * 1024),
        cost_estimate=pl.CostEstimate(
            flops=4 * patches * patches * cols,
            bytes_accessed=8 * patches * cols,
            transcendentals=patches * patches * len(chunk),
        ),
        name="attend",
    )(layer, qkv, *arrived, *given)
    return list(outs)


def unpack_kernel(places, width, *rest):
    parts, out, sems = rest[: len(places)], rest[-2], rest[-1]
    me = lax.axis_index("seq")
    copies = []
    for part, (chunk, slot) in zip(parts, places, strict=True):
        for sample, first, cols, size in spans(chunk):
            start = pl.multiple_of(lax.bitwise_xor(me, slot) * width + first, HD)
            there = out.at[0, sample, :, pl.ds(start, size)]
            copies.append(pltpu.make_async_copy(part.at[:, cols], there, sems.at[len(copies)]))
    for copy in copies:
        copy.start()
    for copy in copies:
        copy.wait()


def unpack(parts, places, width, shape):
    return pl.pallas_call(
        functools.partial(unpack_kernel, places, width),
        out_shape=jax.ShapeDtypeStruct(shape, parts[0].dtype),
        in_specs=[VMEM] * len(parts),
        out_specs=ANY,
        scratch_shapes=[
            pltpu.SemaphoreType.DMA((sum(len(spans(chunk)) for chunk, _ in places),))
        ],
        compiler_params=pltpu.CompilerParams(vmem_limit_bytes=4 * 1024 * 1024),
        name="unpack",
    )(*parts)


def swap(part, slot):
    if slot == 0:
        return part
    return lax.ppermute(part, "seq", [(place, place ^ slot) for place in range(lax.axis_size("seq"))])


def mixed(one, other):
    return [slot for pair in zip(one, other, strict=True) for slot in pair]


def shards(dp_count, seq_count, qkv, master, moment_one, moment_two, grads):
    width = qkv.shape[4] // seq_count
    half = seq_count // 2
    far, near = list(range(half, seq_count)), list(range(1, half))
    turned = far[half // 2 :] + far[: half // 2]
    pairs = [(sample, head) for sample in range(qkv.shape[2]) for head in range(width // HD)]
    cut = len(pairs) - max(1, len(pairs) // 2)
    chunks = [pairs[:cut], pairs[cut:]]
    orders = [
        [turned[0], near[0], turned[1]] + mixed(turned[2:], near[1:]) + [0],
        mixed(far, near + [0]),
    ]
    landed = []
    for chunk, slots in zip(chunks, orders, strict=True):
        parts = [] if landed else [cut_out(qkv, chunk, slots[0], width)]
        parts += pack(qkv, chunk, slots[len(parts) : -1], width)
        landed.append([swap(part, slot) for part, slot in zip(parts, slots[:-1], strict=True)])
    updated, first_moment, second_moment = adamw(master, moment_one, moment_two, grads)
    layer = own_columns(updated.astype(jnp.bfloat16), dp_count, seq_count, width)
    joined, alone = [0] + near[:-1], near[-1]
    made, outs = {}, []
    for turn, (chunk, slots) in enumerate(zip(chunks, orders, strict=True)):
        given = [outs[slot] for slot in joined] if outs else []
        outs = attend(chunk, slots, joined, width, False, layer, qkv, landed[turn], given)
        made.update({(turn, slot): (out, chunk) for slot, out in enumerate(outs)})
    made.update({(1, slot): (outs[slot], pairs) for slot in joined})
    order = [(0, alone)] + [(turn, slot) for turn in range(2) for slot in far]
    order += [(1, slot) for slot in near[1:] + near[:1] + [0]]
    parts = [swap(made[key][0], key[1]) for key in order]
    places = [(made[key][1], key[1]) for key in order]
    attended = unpack(parts, places, width, (1, *qkv.shape[2:]))
    return (attended, updated, first_moment, second_moment)


def solution(mesh):
    placed = (
        P(None, "dp", None, "seq", None),
        P(None, "dp"),
        P(None, "dp"),
        P(None, "dp"),
        P(None, "dp"),
    )
    return jax.shard_map(
        functools.partial(shards, mesh.shape["dp"], mesh.shape["seq"]),
        mesh=mesh,
        in_specs=placed,
        out_specs=(P("dp", None, "seq", None), P(None, "dp"), P(None, "dp"), P(None, "dp")),
        check_vma=False,
    )
```
